32 devices in a mesh: band: 8 (over z, x), mem: 4 (over y, core).
Axes of the slice: x: 2, y: 2, z: 4, core: 2. Of those that a mesh axis runs over, the one named last changes fastest.
Arguments:
- state: float32 [256, 64, 256], P('mem', 'band'), may hold values from -6 to 6
- courant: float32 [2, 64, 256], P(None, 'band'), may hold values from 0.15 to 0.4
- obs_pert: bfloat16 [8, 512, 256], P('band'), may hold values from -8 to 8
- obs_cell: int32 [8, 512], P('band'), may hold values from 0 to 16383, as said below
- block_rows: int32 [8], replicated, may hold values from 64 to 512, as said below
- band_list: int32 [8, 2], P('band'), may hold values from 0 to 7, as said below
Outputs:
- analysis: float32 [256, 64, 256], P('mem', 'band')
The draws below stay inside these ranges and needn't reach their ends.
Inputs may be any that keep to these rules, and one draw needn't show every extreme that they name: `band_list`: row b holds 2 different block numbers, each one of b - 1, b, b + 1 taken modulo 8. `block_rows`: the first that many rows of a block are live. Some block has exactly 512 in every draw. `obs_cell`: the rows of block j lie in latitude rows j * 8 to (j + 1) * 8 - 1; a cell is numbered latitude row times 256 plus longitude.
All inputs are finite; a program needn't handle non-finite values.
Results may differ from the reference program's by a relative error of at most 0.0045.
Values may be sent and summed in bfloat16 or wider, within the bound.
A program may use at most 64 MiB of HBM per device.

```python
import jax
import jax.numpy as jnp
from jax import lax

MEMBERS = 256
ROWS_BAND = 8
LON = 256
STEPS = 6
OBS_ROWS = 512
LIST = 2
DEGREE = 4
BLOCKS = 8
NLAT = 64
N_BAND = 8


def draw_band_list(key, part):
    scores = jax.random.randint(key, (BLOCKS, 3), 0, 1 << 20) * 4 + jnp.arange(3, dtype=jnp.int32)[None, :]
    chosen = jnp.argsort(scores, axis=1, stable=True)[:, :LIST].astype(jnp.int32)
    listed = (jnp.arange(BLOCKS, dtype=jnp.int32)[:, None] + chosen - 1) % BLOCKS
    return listed.astype(jnp.int32)


def draw_block_rows(key, part):
    first_key, second_key = jax.random.split(key)
    counts = jax.random.randint(first_key, (BLOCKS,), OBS_ROWS // 8, OBS_ROWS + 1)
    fullest = jax.random.randint(second_key, (), 0, BLOCKS)
    counts = jnp.where(jnp.arange(BLOCKS, dtype=jnp.int32) == fullest, OBS_ROWS, counts)
    return counts.astype(jnp.int32)


def draw_obs_cell(key, part):
    inside = jax.random.randint(key, (BLOCKS, OBS_ROWS), 0, ROWS_BAND * LON)
    offsets = jnp.arange(BLOCKS, dtype=jnp.int32)[:, None] * (ROWS_BAND * LON)
    return (inside + offsets).astype(jnp.int32)


def steps_of(rng, dims, shards, smallest, largest):
    def one(axis_at, blocks):
        heights = jax.random.uniform(jax.random.fold_in(jax.random.fold_in(rng, 6), axis_at), (blocks,), jnp.float32, smallest / len(shards), largest / len(shards))
        return jnp.repeat(jnp.exp(heights), dims[axis_at] // blocks).reshape((-1,) + (1,) * (len(dims) - axis_at - 1))

    level = one(*shards[0])
    for cut in shards[1:]:
        level = level * one(*cut)
    return level


def normal_values(own_key, shape, deviation, bound, cuts=(), kind=jnp.bfloat16):
    level = steps_of(own_key, shape, cuts, -0.22, 0.18) if cuts else 1.0
    result = jax.random.normal(own_key, shape, jnp.float32) * deviation * level
    return jnp.minimum(jnp.maximum(result, -bound), bound).astype(kind)


def setup_inputs(seed: int = 0) -> dict:
    splits = jax.random.split(jax.random.key(seed), 7)
    return {
        "state": normal_values(splits[0], (MEMBERS, NLAT, LON), 1.0, 6.0, ((0, 4), (1, 8)), jnp.float32),
        "courant": jnp.clip(0.15 + 0.25 * jax.random.uniform(splits[1], (2, NLAT, LON), jnp.float32) ** steps_of(splits[1], (2, NLAT, LON), ((1, 8),), -0.2, 0.2), 0.15, 0.4),
        "obs_pert": normal_values(splits[2], (BLOCKS, OBS_ROWS, MEMBERS), 1.8, 8.0, ((0, 8),)),
        "obs_cell": draw_obs_cell(jax.random.fold_in(splits[6], 71), 0),
        "block_rows": draw_block_rows(jax.random.fold_in(splits[6], 71), 0),
        "band_list": draw_band_list(jax.random.fold_in(splits[6], 71), 0),
    }


DIFFUSION = 0.05
COEFFS = (1.0, -0.5, 0.375, -0.3125, 0.2734375)


def advance_member(tracer, courant):
    northern = jnp.roll(tracer, 1, axis=0)
    southern = jnp.roll(tracer, -1, axis=0)
    western = jnp.roll(tracer, 1, axis=1)
    eastern = jnp.roll(tracer, -1, axis=1)
    saturation = 0.5 + 0.5 * jnp.tanh(tracer)
    return (tracer - courant[0] * saturation * (tracer - northern)
            - courant[1] * saturation * (tracer - western)
            + DIFFUSION * (northern + southern + eastern + western - 4.0 * tracer))


def localization(obs_cells, live_rows, cell_flat, lat_count, lon_count, rows_band, gscale):
    obs_lat = obs_cells // lon_count
    obs_lon = obs_cells % lon_count
    cell_lat = cell_flat // lon_count
    cell_lon = cell_flat % lon_count
    lat_gap = jnp.abs(obs_lat[:, None] - cell_lat[None, :])
    lat_gap = jnp.minimum(lat_gap, lat_count - lat_gap)
    lon_gap = jnp.abs(obs_lon[:, None] - cell_lon[None, :])
    lon_gap = jnp.minimum(lon_gap, lon_count - lon_gap)
    lat_term = lat_gap.astype(jnp.float32) * (1.0 / rows_band)
    lon_term = lon_gap.astype(jnp.float32) * (4.0 / lon_count)
    decay = jnp.exp(-0.5 * (lat_term * lat_term + lon_term * lon_term)) * gscale
    return jnp.where(live_rows[:, None], decay, jnp.zeros_like(decay))


def transform(pert, observed, weight):
    series = pert
    combined = COEFFS[0] * pert
    for power in range(1, DEGREE + 1):
        projected = jnp.dot(observed, series.astype(jnp.bfloat16), preferred_element_type=jnp.float32)
        scaled = (projected * weight).astype(jnp.bfloat16)
        series = lax.dot_general(observed, scaled, (((0,), (0,)), ((), ())), preferred_element_type=jnp.float32)
        combined = combined + COEFFS[power] * series
    return combined


def reference(state, courant, obs_pert, obs_cell, block_rows, band_list):
    def run_member(tracer):
        for section in range(STEPS):
            tracer = advance_member(tracer, courant)
        return tracer

    advected = lax.map(run_member, state)
    band_cells = ROWS_BAND * LON
    gscale = 1.0 / (MEMBERS + LIST * OBS_ROWS)

    def per_band(band_index):
        columns = lax.dynamic_slice_in_dim(advected, band_index * ROWS_BAND, ROWS_BAND, 1)
        columns = columns.reshape(MEMBERS, band_cells)
        average = jnp.mean(columns, axis=0, keepdims=True)
        pert = columns - average
        block_ids = band_list[band_index]
        observed = obs_pert[block_ids].reshape(LIST * OBS_ROWS, MEMBERS)
        obs_cells = obs_cell[block_ids].reshape(LIST * OBS_ROWS)
        live_rows = (jnp.arange(OBS_ROWS, dtype=jnp.int32)[None, :] < block_rows[block_ids][:, None]).reshape(-1)
        cell_flat = band_index * band_cells + jnp.arange(band_cells, dtype=jnp.int32)
        weight = localization(obs_cells, live_rows, cell_flat, NLAT, LON, ROWS_BAND, gscale)
        return average + transform(pert, observed, weight)

    analysed = lax.map(per_band, jnp.arange(N_BAND, dtype=jnp.int32))
    analysed = analysed.reshape(N_BAND, MEMBERS, ROWS_BAND, LON).transpose(1, 0, 2, 3)
    return analysed.reshape(MEMBERS, NLAT, LON)
```

```python
import functools

import jax
import jax.numpy as jnp
from jax import lax
from jax.experimental import pallas as pl
from jax.experimental.pallas import tpu as pltpu
from jax.sharding import PartitionSpec as P

STEPS = 6
LIST = 2
DEGREE = 4
DIFFUSION = 0.05
COEFFS = (1.0, -0.5, 0.375, -0.3125, 0.2734375)
CHUNK = 16
SUB = 8
LANES = 128
MESH = pl.DeviceIdType.MESH


def kernel(
    dims,
    state, courant, cells_in, rows_in, list_in, obs,
    out,
    near, near_cells, near_t, weight,
    halo_send, halo_recv, aux_send, aux_recv, halo, wind,
    adv, ref_send, ref_recv, group_send, group_recv, back_send, back_recv, series, total,
    obs_s, obs_r, cell_s, cell_r, spread_s, spread_r, aux_s, aux_r, halo_s, halo_r,
    ref_s, ref_r, group_s, group_r, back_s, back_r, own_sem,
):
    n_band, n_mem, local, band_rows, lon, obs_rows, halves = dims
    chunks = local // CHUNK
    group = band_rows * lon // n_mem
    width = group // halves
    part = obs_rows // n_mem
    members = local * n_mem
    near_winds = STEPS - 1
    b = lax.axis_index("band")
    m = lax.axis_index("mem")
    bands = (lax.rem(b + n_band - 1, n_band), lax.rem(b + 1, n_band))
    peers = [lax.rem(m + k, n_mem) for k in range(n_mem)]

    barrier = pltpu.get_barrier_semaphore()
    for d in range(2):
        pl.semaphore_signal(barrier, inc=1, device_id={"band": bands[d], "mem": m}, device_id_type=MESH)
    for k in range(1, n_mem):
        pl.semaphore_signal(barrier, inc=1, device_id={"band": b, "mem": peers[k]}, device_id_type=MESH)
    pl.semaphore_wait(barrier, 2 + n_mem - 1)

    def to_band(d, src, dst, ssem, rsem):
        return pltpu.make_async_remote_copy(
            src_ref=src, dst_ref=dst, send_sem=ssem, recv_sem=rsem,
            device_id={"band": bands[d], "mem": m}, device_id_type=MESH,
        )

    def to_peer(k, src, dst, ssem, rsem):
        return pltpu.make_async_remote_copy(
            src_ref=src, dst_ref=dst, send_sem=ssem, recv_sem=rsem,
            device_id={"band": b, "mem": peers[k]}, device_id_type=MESH,
        )

    slots = (2, 0)
    mine = pl.ds(pl.multiple_of(m * part, part), part)

    def obs_copy(d):
        return to_band(d, obs.at[0, mine], near.at[slots[d], mine], obs_s.at[d], obs_r.at[d])

    def cell_copy(d):
        return to_band(d, cells_in, near_cells.at[slots[d]], cell_s.at[d], cell_r.at[d])

    def spread_copy(d, k):
        block = near.at[slots[d], mine]
        return to_peer(k, block, block, spread_s.at[d, k], spread_r.at[d, k])

    def aux_copy(d):
        return to_band(d, aux_send.at[d], aux_recv.at[d], aux_s.at[d], aux_r.at[d])

    def halo_copy(d, c):
        return to_band(d, halo_send.at[d, c], halo_recv.at[d, c], halo_s.at[d, c], halo_r.at[d, c])

    def ref_copy(k):
        if k == 0:
            return pltpu.make_async_copy(ref_send.at[m], ref_recv.at[m], ref_s.at[0])
        return to_peer(k, ref_send.at[peers[k]], ref_recv.at[m], ref_s.at[k], ref_r.at[k])

    def group_copy(c, k):
        if k == 0:
            return pltpu.make_async_copy(group_send.at[m, c], group_recv.at[m, c], group_s.at[c, 0])
        return to_peer(k, group_send.at[peers[k], c], group_recv.at[m, c], group_s.at[c, k], group_r.at[c, k])

    def back_copy(h, k):
        if k == 0:
            return pltpu.make_async_copy(back_send.at[h, m], back_recv.at[h, m], back_s.at[h, 0])
        return to_peer(k, back_send.at[h, peers[k]], back_recv.at[h, m], back_s.at[h, k], back_r.at[h, k])

    for d in range(2):
        cell_copy(d).start()
        obs_copy(d).start()
    own_obs = pltpu.make_async_copy(obs.at[0], near.at[1], own_sem)
    own_obs.start()
    near_cells[1] = cells_in[...]

    @pl.loop(0, local // SUB)
    def _(block):
        span = pl.ds(pl.multiple_of(block * SUB, SUB), SUB)
        adv[:, span] = jnp.swapaxes(state[span], 0, 1)

    def outer_rows(d):
        return range(STEPS) if d == 0 else range(band_rows - STEPS, band_rows)

    base = []
    for row in range(band_rows):
        base.append(jnp.sum(adv[row], axis=0, keepdims=True) * (1.0 / local))
    for d in range(2):
        rows = list(outer_rows(d))
        kept = rows[:near_winds] if d == 0 else rows[STEPS - near_winds:]
        for i, row in enumerate(kept):
            aux_send[d, i : i + 1] = courant[0, row : row + 1]
            aux_send[d, near_winds + i : near_winds + i + 1] = courant[1, row : row + 1]
        for i, row in enumerate(rows):
            aux_send[d, 2 * near_winds + i : 2 * near_winds + i + 1] = base[row]
        aux_copy(d).start()

    @pl.loop(0, chunks)
    def _(c):
        full = pl.ds(pl.multiple_of(c * CHUNK, CHUNK), CHUNK)
        for row in range(band_rows):
            both = (adv[row, full] - base[row]).astype(jnp.bfloat16)
            for d in range(2):
                rows = list(outer_rows(d))
                if row in rows:
                    halo_send[d, c, rows.index(row)] = both
        for d in range(2):
            halo_copy(d, c).start()

    for d in range(2):
        obs_copy(d).wait_recv()
        for k in range(1, n_mem):
            spread_copy(d, k).start()
    for d in range(2):
        cell_copy(d).wait_recv()

    ids = [list_in[0, t] for t in range(LIST)]
    offs = [lax.min(lax.rem(ids[t] - b + 1 + n_band, n_band), 2) for t in range(LIST)]
    gscale = 1.0 / (members + LIST * obs_rows)
    nlat = n_band * band_rows
    for t in range(LIST):
        count = rows_in[ids[t]]
        flat = near_cells[offs[t]]
        lat = lax.div(flat, jnp.int32(lon))
        obs_lon = (flat - lat * lon).astype(jnp.float32)
        obs_lat = lat.astype(jnp.float32)
        for piece in range(obs_rows // LANES):
            span = slice(piece * LANES, (piece + 1) * LANES)
            lat_c = jnp.transpose(jnp.broadcast_to(obs_lat[:, span], (LANES, LANES)))
            lon_c = jnp.transpose(jnp.broadcast_to(obs_lon[:, span], (LANES, LANES)))
            live = lax.broadcasted_iota(jnp.int32, (LANES, LANES), 0) + piece * LANES < count
            for block in range(group // LANES):
                first = m * group + block * LANES
                row = first // lon
                cell_lat = (b * band_rows + row).astype(jnp.float32)
                cell_lon = (first - row * lon).astype(jnp.float32) + lax.broadcasted_iota(
                    jnp.int32, (LANES, LANES), 1
                ).astype(jnp.float32)
                lat_gap = jnp.abs(lat_c - cell_lat)
                lat_gap = jnp.minimum(lat_gap, nlat - lat_gap)
                lon_gap = jnp.abs(lon_c - cell_lon)
                lon_gap = jnp.minimum(lon_gap, lon - lon_gap)
                lat_term = lat_gap * (1.0 / band_rows)
                lon_term = lon_gap * (4.0 / lon)
                decay = jnp.exp(-0.5 * (lat_term * lat_term + lon_term * lon_term)) * gscale
                weight[t, span, block * LANES : (block + 1) * LANES] = jnp.where(
                    live, decay, jnp.zeros_like(decay)
                )

    for d in range(2):
        aux_copy(d).wait_recv()
    for part_at in range(2):
        lead = near_winds * part_at
        for i in range(near_winds):
            wind[part_at, i] = jnp.broadcast_to(0.5 * aux_recv[1, lead + i : lead + i + 1], (SUB, lon))
            wind[part_at, near_winds + band_rows + i] = jnp.broadcast_to(
                0.5 * aux_recv[0, lead + i : lead + i + 1], (SUB, lon)
            )
        for i in range(band_rows):
            wind[part_at, near_winds + i] = jnp.broadcast_to(0.5 * courant[part_at, i : i + 1], (SUB, lon))

    def advect(c):
        for d in range(2):
            halo_copy(d, c).wait_recv()
        for d in range(2):
            for i in range(STEPS):
                at = 2 * near_winds + i
                halo[1 - d, i] = halo_recv[d, c, i].astype(jnp.float32) + aux_recv[d, at : at + 1]

        @pl.loop(0, CHUNK // SUB)
        def _(s):
            span = pl.ds(pl.multiple_of(s * SUB, SUB), SUB)
            q = [halo[0, i, span] for i in range(STEPS)]
            full = pl.ds(pl.multiple_of(c * CHUNK + s * SUB, SUB), SUB)
            q += [adv[row, full] for row in range(band_rows)]
            q += [halo[1, i, span] for i in range(STEPS)]
            for step in range(STEPS):
                new = []
                for i in range(1, len(q) - 1):
                    now, north, south = q[i], q[i - 1], q[i + 1]
                    west = pltpu.roll(now, 1, 1)
                    east = pltpu.roll(now, lon - 1, 1)
                    at = i - 1 + step
                    rise = wind[0, at] * (now - north) + wind[1, at] * (now - west)
                    near4 = (north + south) + (east + west)
                    new.append(
                        (1.0 - 4.0 * DIFFUSION) * now + DIFFUSION * near4 - (1.0 + jnp.tanh(now)) * rise
                    )
                q = new
            for row in range(band_rows):
                adv[row, full] = q[row]

    def pieces():
        for row in range(band_rows):
            for lane in range(0, lon, LANES):
                cell = row * lon + lane
                yield row, slice(lane, lane + LANES), cell // group, cell % group

    def regroup(c):
        full = pl.ds(pl.multiple_of(c * CHUNK, CHUNK), CHUNK)
        for row, lanes, g, at in pieces():
            diff = adv[row, full, lanes] - ref_send[g, :, at : at + LANES]
            group_send[g, c, :, at : at + LANES] = diff.astype(jnp.bfloat16)
        for k in range(n_mem):
            group_copy(c, k).start()

    advect(0)
    for row, lanes, g, at in pieces():
        ref_send[g, :, at : at + LANES] = jnp.mean(adv[row, :CHUNK, lanes], axis=0, keepdims=True)
    for k in range(n_mem):
        ref_copy(k).start()
    regroup(0)

    @pl.loop(1, chunks)
    def _(c):
        advect(c)
        regroup(c)

    own_obs.wait()
    for d in range(2):
        for k in range(1, n_mem):
            spread_copy(d, k).wait_recv()
    for t in range(LIST):
        near_t[t] = jnp.transpose(near[offs[t]])

    for k in range(n_mem):
        copies = [ref_copy(k)] + [group_copy(c, k) for c in range(chunks)]
        for copy in copies:
            copy.wait() if k == 0 else copy.wait_recv()
    average = jnp.zeros((1, group), jnp.float32)
    for j in range(n_mem):
        added = jnp.zeros((CHUNK, group), jnp.float32)
        for c in range(chunks):
            added = added + group_recv[j, c].astype(jnp.float32)
        average = average + jnp.sum(added, axis=0, keepdims=True) + local * ref_recv[j]
    average = average * (1.0 / members)
    for j in range(n_mem):
        shift = ref_recv[j] - average
        for c in range(chunks):
            start = j * local + c * CHUNK
            pert = group_recv[j, c].astype(jnp.float32) + shift
            series[start : start + CHUNK] = pert.astype(jnp.bfloat16)

    for h in range(halves):
        lanes = slice(h * width, (h + 1) * width)
        for power in range(1, DEGREE + 1):
            held = series[:, lanes]
            result = None
            for t in range(LIST):
                projected = jnp.dot(near[offs[t]], held, preferred_element_type=jnp.float32)
                scaled = (projected * weight[t, :, lanes]).astype(jnp.bfloat16)
                term = jnp.dot(near_t[t], scaled, preferred_element_type=jnp.float32)
                result = term if result is None else result + term
            if power < DEGREE:
                series[:, lanes] = result.astype(jnp.bfloat16)
            if power == 1:
                total[...] = COEFFS[power] * result
            elif power < DEGREE:
                total[...] += COEFFS[power] * result
            else:
                last = (total[...] + COEFFS[power] * result).astype(jnp.bfloat16)
                for j in range(n_mem):
                    back_send[h, j] = last[j * local : (j + 1) * local]
        for k in range(n_mem):
            back_copy(h, k).start()

    for h in range(halves):
        for k in range(n_mem):
            copy = back_copy(h, k)
            copy.wait() if k == 0 else copy.wait_recv()
        for row, lanes, g, at in pieces():
            if at // width != h:
                continue
            off = at - h * width
            adv[row, :, lanes] += back_recv[h, g, :, off : off + LANES].astype(jnp.float32)

    @pl.loop(0, local // SUB)
    def _(block):
        span = pl.ds(pl.multiple_of(block * SUB, SUB), SUB)
        out[span] = jnp.swapaxes(adv[:, span], 0, 1)

    for d in range(2):
        cell_copy(d).wait_send()
        obs_copy(d).wait_send()
        aux_copy(d).wait_send()
        for c in range(chunks):
            halo_copy(d, c).wait_send()
        for k in range(1, n_mem):
            spread_copy(d, k).wait_send()
    for k in range(1, n_mem):
        ref_copy(k).wait_send()
        for c in range(chunks):
            group_copy(c, k).wait_send()
        for h in range(halves):
            back_copy(h, k).wait_send()


def shards(state, courant, obs_pert, obs_cell, block_rows, band_list):
    local, band_rows, lon = state.shape
    n_band = lax.axis_size("band")
    n_mem = lax.axis_size("mem")
    obs_rows, members = obs_pert.shape[1:]
    group = band_rows * lon // n_mem
    halves = 2 if group >= 4 * LANES else 1
    width = group // halves
    chunks = local // CHUNK
    bf16, f32 = jnp.bfloat16, jnp.float32
    dma = pltpu.SemaphoreType.DMA
    vmem = pl.BlockSpec(memory_space=pltpu.VMEM)
    smem = pl.BlockSpec(memory_space=pltpu.SMEM)
    return pl.pallas_call(
        functools.partial(kernel, (n_band, n_mem, local, band_rows, lon, obs_rows, halves)),
        out_shape=jax.ShapeDtypeStruct(state.shape, f32),
        in_specs=[vmem, vmem, vmem, smem, smem, pl.BlockSpec(memory_space=pl.ANY)],
        out_specs=vmem,
        scratch_shapes=[
            pltpu.VMEM((3, obs_rows, members), bf16),
            pltpu.VMEM((3, 1, obs_rows), jnp.int32),
            pltpu.VMEM((LIST, members, obs_rows), bf16),
            pltpu.VMEM((LIST, obs_rows, group), f32),
            pltpu.VMEM((2, chunks, STEPS, CHUNK, lon), bf16),
            pltpu.VMEM((2, chunks, STEPS, CHUNK, lon), bf16),
            pltpu.VMEM((2, 16, lon), f32),
            pltpu.VMEM((2, 16, lon), f32),
            pltpu.VMEM((2, STEPS, CHUNK, lon), f32),
            pltpu.VMEM((2, band_rows + 2 * (STEPS - 1), SUB, lon), f32),
            pltpu.VMEM((band_rows, local, lon), f32),
            pltpu.VMEM((n_mem, 1, group), f32),
            pltpu.VMEM((n_mem, 1, group), f32),
            pltpu.VMEM((n_mem, chunks, CHUNK, group), bf16),
            pltpu.VMEM((n_mem, chunks, CHUNK, group), bf16),
            pltpu.VMEM((halves, n_mem, local, width), bf16),
            pltpu.VMEM((halves, n_mem, local, width), bf16),
            pltpu.VMEM((members, group), bf16),
            pltpu.VMEM((members, width), f32),
            dma((2,)), dma((2,)), dma((2,)), dma((2,)),
            dma((2, n_mem)), dma((2, n_mem)),
            dma((2,)), dma((2,)),
            dma((2, chunks)), dma((2, chunks)),
            dma((n_mem,)), dma((n_mem,)),
            dma((chunks, n_mem)), dma((chunks, n_mem)),
            dma((halves, n_mem)), dma((halves, n_mem)),
            dma(()),
        ],
        compiler_params=pltpu.CompilerParams(
            collective_id=0, has_side_effects=True, vmem_limit_bytes=40 * 1024 * 1024
        ),
    )(state, courant, obs_cell, block_rows, band_list, obs_pert)


def solution(mesh):
    return jax.shard_map(
        shards,
        mesh=mesh,
        in_specs=(
            P("mem", "band", None),
            P(None, "band", None),
            P("band", None, None),
            P("band", None),
            P(),
            P("band", None),
        ),
        out_specs=P("mem", "band", None),
        check_vma=False,
    )
```

```python
import functools

import jax
import jax.numpy as jnp
from jax import lax
from jax.experimental import pallas as pl
from jax.experimental.pallas import tpu as pltpu
from jax.sharding import PartitionSpec as P

STEPS = 6
LIST = 2
DEGREE = 4
DIFFUSION = 0.05
COEFFS = (1.0, -0.5, 0.375, -0.3125, 0.2734375)
CHUNK = 16
SUB = 8
LANES = 128
MESH = pl.DeviceIdType.MESH


def kernel(
    dims,
    state_in, courant_in, cells_in, rows_list, list_list, obs,
    out,
    state, courant, rows_in, list_in,
    near, near_cells, near_t, weight,
    halo_send, halo_recv, aux_send, aux_recv, halo, wind,
    adv, ref_send, ref_recv, group_send, group_recv, back_send, back_recv, series, total,
    obs_s, obs_r, cell_s, cell_r, spread_s, spread_r, aux_s, aux_r, halo_s, halo_r,
    ref_s, ref_r, group_s, group_r, back_s, back_r, own_sem, out_sem,
):
    n_band, n_mem, local, band_rows, lon, obs_rows, halves = dims
    chunks = local // CHUNK
    group = band_rows * lon // n_mem
    width = group // halves
    part = obs_rows // n_mem
    members = local * n_mem
    near_winds = STEPS - 1
    b = lax.axis_index("band")
    m = lax.axis_index("mem")
    bands = (lax.rem(b + n_band - 1, n_band), lax.rem(b + 1, n_band))
    chip, core = m // 2, m % 2
    chips = [lax.rem(chip + k, n_mem // 2) for k in range(n_mem // 2)]
    peers = [chips[k // 2] * 2 + lax.rem(core + k % 2, 2) for k in range(n_mem)]
    far_first = list(range(n_mem))[::-1]

    loads = [
        pltpu.make_async_copy(src, dst, own_sem.at[i])
        for i, (src, dst) in enumerate(
            (
                (state_in, state),
                (courant_in, courant),
                (cells_in, near_cells.at[1]),
                (rows_list, rows_in),
                (list_list, list_in),
                (obs.at[0], near.at[1]),
            )
        )
    ]
    for load in loads:
        load.start()
    barrier = pltpu.get_barrier_semaphore()
    for d in range(2):
        pl.semaphore_signal(barrier, inc=1, device_id={"band": bands[d], "mem": m}, device_id_type=MESH)
    for k in range(1, n_mem):
        pl.semaphore_signal(barrier, inc=1, device_id={"band": b, "mem": peers[k]}, device_id_type=MESH)
    pl.semaphore_wait(barrier, 2 + n_mem - 1)

    def to_band(d, src, dst, ssem, rsem):
        return pltpu.make_async_remote_copy(
            src_ref=src, dst_ref=dst, send_sem=ssem, recv_sem=rsem,
            device_id={"band": bands[d], "mem": m}, device_id_type=MESH,
        )

    def to_peer(k, src, dst, ssem, rsem):
        return pltpu.make_async_remote_copy(
            src_ref=src, dst_ref=dst, send_sem=ssem, recv_sem=rsem,
            device_id={"band": b, "mem": peers[k]}, device_id_type=MESH,
        )

    def out_copy(block):
        span = pl.ds(pl.multiple_of(block * SUB, SUB), SUB)
        return pltpu.make_async_copy(state.at[span], out.at[span], out_sem.at[block])

    slots = (2, 0)
    mine = pl.ds(pl.multiple_of(m * part, part), part)

    def obs_copy(d):
        return to_band(d, obs.at[0, mine], near.at[slots[d], mine], obs_s.at[d], obs_r.at[d])

    def cell_copy(d):
        return to_band(d, cells_in, near_cells.at[slots[d]], cell_s.at[d], cell_r.at[d])

    def spread_copy(d, k):
        block = near.at[slots[d], mine]
        return to_peer(k, block, block, spread_s.at[d, k], spread_r.at[d, k])

    def aux_copy(d):
        return to_band(d, aux_send.at[d], aux_recv.at[d], aux_s.at[d], aux_r.at[d])

    def halo_copy(d, c):
        return to_band(d, halo_send.at[d, c], halo_recv.at[d, c], halo_s.at[d, c], halo_r.at[d, c])

    def ref_copy(k):
        if k == 0:
            return pltpu.make_async_copy(ref_send.at[m], ref_recv.at[m], ref_s.at[0])
        return to_peer(k, ref_send.at[peers[k]], ref_recv.at[m], ref_s.at[k], ref_r.at[k])

    def group_copy(c, k):
        if k == 0:
            return pltpu.make_async_copy(group_send.at[m, c], group_recv.at[m, c], group_s.at[c, 0])
        return to_peer(k, group_send.at[peers[k], c], group_recv.at[m, c], group_s.at[c, k], group_r.at[c, k])

    def back_copy(h, k):
        src = back_send.at[h, peers[k]]
        if k == 0:
            return pltpu.make_async_copy(src, back_recv.at[h, m], back_s.at[h, 0])
        return to_peer(k, src, back_recv.at[h, m], back_s.at[h, k], back_r.at[h, k])

    for d in range(2):
        cell_copy(d).start()
        obs_copy(d).start()
    for load in loads[:2]:
        load.wait()

    @pl.loop(0, local // SUB)
    def _(block):
        span = pl.ds(pl.multiple_of(block * SUB, SUB), SUB)
        adv[:, span] = jnp.swapaxes(state[span], 0, 1)

    def outer_rows(d):
        return range(STEPS) if d == 0 else range(band_rows - STEPS, band_rows)

    base = []
    for row in range(band_rows):
        base.append(jnp.sum(adv[row], axis=0, keepdims=True) * (1.0 / local))
    for d in range(2):
        rows = list(outer_rows(d))
        kept = rows[:near_winds] if d == 0 else rows[STEPS - near_winds:]
        for i, row in enumerate(kept):
            aux_send[d, i : i + 1] = courant[0, row : row + 1]
            aux_send[d, near_winds + i : near_winds + i + 1] = courant[1, row : row + 1]
        for i, row in enumerate(rows):
            aux_send[d, 2 * near_winds + i : 2 * near_winds + i + 1] = base[row]
        aux_copy(d).start()

    @pl.loop(0, chunks)
    def _(c):
        full = pl.ds(pl.multiple_of(c * CHUNK, CHUNK), CHUNK)
        for row in range(band_rows):
            both = (adv[row, full] - base[row]).astype(jnp.bfloat16)
            for d in range(2):
                rows = list(outer_rows(d))
                if row in rows:
                    halo_send[d, c, rows.index(row)] = both
        for d in range(2):
            halo_copy(d, c).start()

    for d in range(2):
        obs_copy(d).wait_recv()
        for k in far_first[:-1]:
            spread_copy(d, k).start()
    for d in range(2):
        cell_copy(d).wait_recv()

    for load in loads[2:5]:
        load.wait()

    ids = [list_in[0, t] for t in range(LIST)]
    offs = [lax.min(lax.rem(ids[t] - b + 1 + n_band, n_band), 2) for t in range(LIST)]
    gscale = 1.0 / (members + LIST * obs_rows)
    nlat = n_band * band_rows
    for t in range(LIST):
        count = rows_in[ids[t]]
        flat = near_cells[offs[t]]
        lat = lax.div(flat, jnp.int32(lon))
        obs_lon = (flat - lat * lon).astype(jnp.float32)
        obs_lat = lat.astype(jnp.float32)
        for piece in range(obs_rows // LANES):
            span = slice(piece * LANES, (piece + 1) * LANES)
            lat_c = jnp.transpose(jnp.broadcast_to(obs_lat[:, span], (LANES, LANES)))
            lon_c = jnp.transpose(jnp.broadcast_to(obs_lon[:, span], (LANES, LANES)))
            live = lax.broadcasted_iota(jnp.int32, (LANES, LANES), 0) + piece * LANES < count
            for block in range(group // LANES):
                first = m * group + block * LANES
                row = first // lon
                cell_lat = (b * band_rows + row).astype(jnp.float32)
                cell_lon = (first - row * lon).astype(jnp.float32) + lax.broadcasted_iota(
                    jnp.int32, (LANES, LANES), 1
                ).astype(jnp.float32)
                lat_gap = jnp.abs(lat_c - cell_lat)
                lat_gap = jnp.minimum(lat_gap, nlat - lat_gap)
                lon_gap = jnp.abs(lon_c - cell_lon)
                lon_gap = jnp.minimum(lon_gap, lon - lon_gap)
                lat_term = lat_gap * (1.0 / band_rows)
                lon_term = lon_gap * (4.0 / lon)
                decay = jnp.exp(-0.5 * (lat_term * lat_term + lon_term * lon_term)) * gscale
                weight[t, span, block * LANES : (block + 1) * LANES] = jnp.where(
                    live, decay, jnp.zeros_like(decay)
                )

    for d in range(2):
        aux_copy(d).wait_recv()
    for part_at in range(2):
        lead = near_winds * part_at
        for i in range(near_winds):
            wind[part_at, i] = jnp.broadcast_to(0.5 * aux_recv[1, lead + i : lead + i + 1], (SUB, lon))
            wind[part_at, near_winds + band_rows + i] = jnp.broadcast_to(
                0.5 * aux_recv[0, lead + i : lead + i + 1], (SUB, lon)
            )
        for i in range(band_rows):
            wind[part_at, near_winds + i] = jnp.broadcast_to(0.5 * courant[part_at, i : i + 1], (SUB, lon))

    def advect(c):
        for d in range(2):
            halo_copy(d, c).wait_recv()
        for d in range(2):
            for i in range(STEPS):
                at = 2 * near_winds + i
                halo[1 - d, i] = halo_recv[d, c, i].astype(jnp.float32) + aux_recv[d, at : at + 1]

        @pl.loop(0, CHUNK // SUB)
        def _(s):
            span = pl.ds(pl.multiple_of(s * SUB, SUB), SUB)
            q = [halo[0, i, span] for i in range(STEPS)]
            full = pl.ds(pl.multiple_of(c * CHUNK + s * SUB, SUB), SUB)
            q += [adv[row, full] for row in range(band_rows)]
            q += [halo[1, i, span] for i in range(STEPS)]
            for step in range(STEPS):
                new = []
                for i in range(1, len(q) - 1):
                    now, north, south = q[i], q[i - 1], q[i + 1]
                    west = pltpu.roll(now, 1, 1)
                    east = pltpu.roll(now, lon - 1, 1)
                    at = i - 1 + step
                    rise = wind[0, at] * (now - north) + wind[1, at] * (now - west)
                    near4 = (north + south) + (east + west)
                    new.append(
                        (1.0 - 4.0 * DIFFUSION) * now + DIFFUSION * near4 - (1.0 + jnp.tanh(now)) * rise
                    )
                q = new
            for row in range(band_rows):
                adv[row, full] = q[row]

    def pieces():
        for row in range(band_rows):
            for lane in range(0, lon, LANES):
                cell = row * lon + lane
                yield row, slice(lane, lane + LANES), cell // group, cell % group

    def regroup(c):
        full = pl.ds(pl.multiple_of(c * CHUNK, CHUNK), CHUNK)
        for row, lanes, g, at in pieces():
            diff = adv[row, full, lanes] - ref_send[g, :, at : at + LANES]
            group_send[g, c, :, at : at + LANES] = diff.astype(jnp.bfloat16)
        for k in far_first:
            group_copy(c, k).start()

    advect(0)
    for row, lanes, g, at in pieces():
        ref_send[g, :, at : at + LANES] = jnp.mean(adv[row, :CHUNK, lanes], axis=0, keepdims=True)
    for k in range(n_mem):
        ref_copy(k).start()
    regroup(0)

    @pl.loop(1, chunks)
    def _(c):
        advect(c)
        regroup(c)

    loads[5].wait()
    for d in range(2):
        for k in range(1, n_mem):
            spread_copy(d, k).wait_recv()
    for t in range(LIST):
        near_t[t] = jnp.transpose(near[offs[t]])

    for k in range(n_mem):
        copies = [ref_copy(k)] + [group_copy(c, k) for c in range(chunks)]
        for copy in copies:
            copy.wait() if k == 0 else copy.wait_recv()
    average = jnp.zeros((1, group), jnp.float32)
    for j in range(n_mem):
        added = jnp.zeros((CHUNK, group), jnp.float32)
        for c in range(chunks):
            added = added + group_recv[j, c].astype(jnp.float32)
        average = average + jnp.sum(added, axis=0, keepdims=True) + local * ref_recv[j]
    average = average * (1.0 / members)
    for j in range(n_mem):
        shift = ref_recv[j] - average
        for c in range(chunks):
            start = j * local + c * CHUNK
            pert = group_recv[j, c].astype(jnp.float32) + shift
            series[start : start + CHUNK] = pert.astype(jnp.bfloat16)

    def scaled(t, lanes):
        projected = jnp.dot(near[offs[t]], series[:, lanes], preferred_element_type=jnp.float32)
        return (projected * weight[t, :, lanes]).astype(jnp.bfloat16)

    for power in range(1, DEGREE):
        result = None
        for t in range(LIST):
            term = jnp.dot(near_t[t], scaled(t, slice(0, group)), preferred_element_type=jnp.float32)
            result = term if result is None else result + term
        series[...] = result.astype(jnp.bfloat16)
        if power == 1:
            total[...] = COEFFS[power] * result
        else:
            total[...] += COEFFS[power] * result
    for h in range(halves):
        lanes = slice(h * width, (h + 1) * width)
        last = [scaled(t, lanes) for t in range(LIST)]
        for at in reversed(range(n_mem // 2)):
            rows = pl.ds(pl.multiple_of(chips[at] * (2 * local), 2 * local), 2 * local)
            result = None
            for t in range(LIST):
                term = jnp.dot(near_t[t, rows], last[t], preferred_element_type=jnp.float32)
                result = term if result is None else result + term
            result = (total[rows, lanes] + COEFFS[DEGREE] * result).astype(jnp.bfloat16)
            for j in range(2):
                back_send[h, chips[at] * 2 + j] = result[j * local : (j + 1) * local]
            for k in (2 * at + 1, 2 * at):
                back_copy(h, k).start()

    for h in range(halves):
        for k in range(n_mem):
            copy = back_copy(h, k)
            copy.wait() if k == 0 else copy.wait_recv()
        for row, lanes, g, at in pieces():
            if at // width != h:
                continue
            off = at - h * width
            adv[row, :, lanes] += back_recv[h, g, :, off : off + LANES].astype(jnp.float32)

    @pl.loop(0, local // SUB)
    def _(block):
        span = pl.ds(pl.multiple_of(block * SUB, SUB), SUB)
        state[span] = jnp.swapaxes(adv[:, span], 0, 1)
        out_copy(block).start()

    @pl.loop(0, local // SUB)
    def _(block):
        out_copy(block).wait()

    for d in range(2):
        cell_copy(d).wait_send()
        obs_copy(d).wait_send()
        aux_copy(d).wait_send()
        for c in range(chunks):
            halo_copy(d, c).wait_send()
        for k in range(1, n_mem):
            spread_copy(d, k).wait_send()
    for k in range(1, n_mem):
        ref_copy(k).wait_send()
        for c in range(chunks):
            group_copy(c, k).wait_send()
        for h in range(halves):
            back_copy(h, k).wait_send()


def shards(state, courant, obs_pert, obs_cell, block_rows, band_list):
    local, band_rows, lon = state.shape
    n_band = lax.axis_size("band")
    n_mem = lax.axis_size("mem")
    obs_rows, members = obs_pert.shape[1:]
    group = band_rows * lon // n_mem
    halves = 2 if group >= 4 * LANES else 1
    width = group // halves
    chunks = local // CHUNK
    bf16, f32 = jnp.bfloat16, jnp.float32
    dma = pltpu.SemaphoreType.DMA
    return pl.pallas_call(
        functools.partial(kernel, (n_band, n_mem, local, band_rows, lon, obs_rows, halves)),
        out_shape=jax.ShapeDtypeStruct(state.shape, f32),
        in_specs=[pl.BlockSpec(memory_space=pltpu.HBM)] * 6,
        out_specs=pl.BlockSpec(memory_space=pltpu.HBM),
        scratch_shapes=[
            pltpu.VMEM(state.shape, f32),
            pltpu.VMEM(courant.shape, f32),
            pltpu.SMEM(block_rows.shape, jnp.int32),
            pltpu.SMEM(band_list.shape, jnp.int32),
            pltpu.VMEM((3, obs_rows, members), bf16),
            pltpu.VMEM((3, 1, obs_rows), jnp.int32),
            pltpu.VMEM((LIST, members, obs_rows), bf16),
            pltpu.VMEM((LIST, obs_rows, group), f32),
            pltpu.VMEM((2, chunks, STEPS, CHUNK, lon), bf16),
            pltpu.VMEM((2, chunks, STEPS, CHUNK, lon), bf16),
            pltpu.VMEM((2, 16, lon), f32),
            pltpu.VMEM((2, 16, lon), f32),
            pltpu.VMEM((2, STEPS, CHUNK, lon), f32),
            pltpu.VMEM((2, band_rows + 2 * (STEPS - 1), SUB, lon), f32),
            pltpu.VMEM((band_rows, local, lon), f32),
            pltpu.VMEM((n_mem, 1, group), f32),
            pltpu.VMEM((n_mem, 1, group), f32),
            pltpu.VMEM((n_mem, chunks, CHUNK, group), bf16),
            pltpu.VMEM((n_mem, chunks, CHUNK, group), bf16),
            pltpu.VMEM((halves, n_mem, local, width), bf16),
            pltpu.VMEM((halves, n_mem, local, width), bf16),
            pltpu.VMEM((members, group), bf16),
            pltpu.VMEM((members, group), f32),
            dma((2,)), dma((2,)), dma((2,)), dma((2,)),
            dma((2, n_mem)), dma((2, n_mem)),
            dma((2,)), dma((2,)),
            dma((2, chunks)), dma((2, chunks)),
            dma((n_mem,)), dma((n_mem,)),
            dma((chunks, n_mem)), dma((chunks, n_mem)),
            dma((halves, n_mem)), dma((halves, n_mem)),
            dma((6,)),
            dma((local // SUB,)),
        ],
        compiler_params=pltpu.CompilerParams(
            collective_id=0, has_side_effects=True, vmem_limit_bytes=62 * 1024 * 1024
        ),
    )(state, courant, obs_cell, block_rows, band_list, obs_pert)


def solution(mesh):
    return jax.shard_map(
        shards,
        mesh=mesh,
        in_specs=(
            P("mem", "band", None),
            P(None, "band", None),
            P("band", None, None),
            P("band", None),
            P(),
            P("band", None),
        ),
        out_specs=P("mem", "band", None),
        check_vma=False,
    )
```

```python
import functools

import jax
import jax.numpy as jnp
from jax import lax
from jax.experimental import pallas as pl
from jax.experimental.pallas import tpu as pltpu
from jax.sharding import PartitionSpec as P

STEPS = 6
LIST = 2
DEGREE = 4
DIFFUSION = 0.05
COEFFS = (1.0, -0.5, 0.375, -0.3125, 0.2734375)
CHUNK = 16
SUB = 8
LANES = 128
MESH = pl.DeviceIdType.MESH


def kernel(
    dims,
    state_in, courant_in, cells_in, rows_list, list_list, obs,
    out,
    state, courant, rows_in, list_in,
    near, near_cells, near_t, weight,
    halo_send, halo_recv, aux_send, aux_recv, halo, wind,
    adv, ref_send, ref_recv, group_send, group_recv, back_send, back_recv, series, total,
    obs_s, obs_r, cell_s, cell_r, spread_s, spread_r, aux_s, aux_r, halo_s, halo_r,
    ref_s, ref_r, group_s, group_r, back_s, back_r, own_sem, out_sem,
):
    n_band, n_mem, local, band_rows, lon, obs_rows, halves = dims
    chunks = local // CHUNK
    group = band_rows * lon // n_mem
    width = group // halves
    part = obs_rows // n_mem
    members = local * n_mem
    near_winds = STEPS - 1
    b = lax.axis_index("band")
    m = lax.axis_index("mem")
    bands = (lax.rem(b + n_band - 1, n_band), lax.rem(b + 1, n_band))
    chip, core = m // 2, m % 2
    chips = [lax.rem(chip + k, n_mem // 2) for k in range(n_mem // 2)]
    peers = [chips[k // 2] * 2 + lax.rem(core + k % 2, 2) for k in range(n_mem)]
    far_first = list(range(n_mem))[::-1]

    loads = [
        pltpu.make_async_copy(src, dst, own_sem.at[i])
        for i, (src, dst) in enumerate(
            (
                (state_in, state),
                (courant_in, courant),
                (cells_in, near_cells.at[1]),
                (rows_list, rows_in),
                (list_list, list_in),
                (obs.at[0], near.at[1]),
            )
        )
    ]
    for load in loads:
        load.start()
    barrier = pltpu.get_barrier_semaphore()
    for d in range(2):
        pl.semaphore_signal(barrier, inc=1, device_id={"band": bands[d], "mem": m}, device_id_type=MESH)
    for k in range(1, n_mem):
        pl.semaphore_signal(barrier, inc=1, device_id={"band": b, "mem": peers[k]}, device_id_type=MESH)
    pl.semaphore_wait(barrier, 2 + n_mem - 1)

    def to_band(d, src, dst, ssem, rsem):
        return pltpu.make_async_remote_copy(
            src_ref=src, dst_ref=dst, send_sem=ssem, recv_sem=rsem,
            device_id={"band": bands[d], "mem": m}, device_id_type=MESH,
        )

    def to_peer(k, src, dst, ssem, rsem):
        return pltpu.make_async_remote_copy(
            src_ref=src, dst_ref=dst, send_sem=ssem, recv_sem=rsem,
            device_id={"band": b, "mem": peers[k]}, device_id_type=MESH,
        )

    def out_copy(block):
        span = pl.ds(pl.multiple_of(block * SUB, SUB), SUB)
        return pltpu.make_async_copy(state.at[span], out.at[span], out_sem.at[block])

    slots = (2, 0)
    mine = pl.ds(pl.multiple_of(m * part, part), part)

    def obs_copy(d):
        return to_band(d, obs.at[0, mine], near.at[slots[d], mine], obs_s.at[d], obs_r.at[d])

    def cell_copy(d):
        return to_band(d, cells_in, near_cells.at[slots[d]], cell_s.at[d], cell_r.at[d])

    def spread_copy(d, k):
        block = near.at[slots[d], mine]
        return to_peer(k, block, block, spread_s.at[d, k], spread_r.at[d, k])

    def aux_copy(d):
        return to_band(d, aux_send.at[d], aux_recv.at[d], aux_s.at[d], aux_r.at[d])

    def halo_copy(d, c):
        return to_band(d, halo_send.at[d, c], halo_recv.at[d, c], halo_s.at[d, c], halo_r.at[d, c])

    def ref_copy(k):
        if k == 0:
            return pltpu.make_async_copy(ref_send.at[m], ref_recv.at[m], ref_s.at[0])
        return to_peer(k, ref_send.at[peers[k]], ref_recv.at[m], ref_s.at[k], ref_r.at[k])

    def group_copy(c, k):
        if k == 0:
            return pltpu.make_async_copy(group_send.at[m, c], group_recv.at[m, c], group_s.at[c, 0])
        return to_peer(k, group_send.at[peers[k], c], group_recv.at[m, c], group_s.at[c, k], group_r.at[c, k])

    def back_copy(h, k):
        src = back_send.at[h, peers[k]]
        if k == 0:
            return pltpu.make_async_copy(src, back_recv.at[h, m], back_s.at[h, 0])
        return to_peer(k, src, back_recv.at[h, m], back_s.at[h, k], back_r.at[h, k])

    for d in range(2):
        cell_copy(d).start()
        obs_copy(d).start()
    for load in loads[:2]:
        load.wait()

    @pl.loop(0, local // SUB)
    def _(block):
        span = pl.ds(pl.multiple_of(block * SUB, SUB), SUB)
        adv[:, span] = jnp.swapaxes(state[span], 0, 1)

    def outer_rows(d):
        return range(STEPS) if d == 0 else range(band_rows - STEPS, band_rows)

    base = []
    for row in range(band_rows):
        base.append(jnp.sum(adv[row], axis=0, keepdims=True) * (1.0 / local))
    for d in range(2):
        rows = list(outer_rows(d))
        kept = rows[:near_winds] if d == 0 else rows[STEPS - near_winds:]
        for i, row in enumerate(kept):
            aux_send[d, i : i + 1] = courant[0, row : row + 1]
            aux_send[d, near_winds + i : near_winds + i + 1] = courant[1, row : row + 1]
        for i, row in enumerate(rows):
            aux_send[d, 2 * near_winds + i : 2 * near_winds + i + 1] = base[row]
        aux_copy(d).start()

    @pl.loop(0, chunks)
    def _(c):
        full = pl.ds(pl.multiple_of(c * CHUNK, CHUNK), CHUNK)
        for row in range(band_rows):
            both = (adv[row, full] - base[row]).astype(jnp.bfloat16)
            for d in range(2):
                rows = list(outer_rows(d))
                if row in rows:
                    halo_send[d, c, rows.index(row)] = both
        for d in range(2):
            halo_copy(d, c).start()

    for d in range(2):
        obs_copy(d).wait_recv()
        for k in far_first[:-1]:
            spread_copy(d, k).start()
    for d in range(2):
        cell_copy(d).wait_recv()

    for load in loads[2:5]:
        load.wait()

    ids = [list_in[0, t] for t in range(LIST)]
    offs = [lax.min(lax.rem(ids[t] - b + 1 + n_band, n_band), 2) for t in range(LIST)]
    gscale = 1.0 / (members + LIST * obs_rows)
    nlat = n_band * band_rows
    for t in range(LIST):
        count = rows_in[ids[t]]
        flat = near_cells[offs[t]]
        lat = lax.div(flat, jnp.int32(lon))
        obs_lon = (flat - lat * lon).astype(jnp.float32)
        obs_lat = lat.astype(jnp.float32)
        for piece in range(obs_rows // LANES):
            span = slice(piece * LANES, (piece + 1) * LANES)
            lat_c = jnp.transpose(jnp.broadcast_to(obs_lat[:, span], (LANES, LANES)))
            lon_c = jnp.transpose(jnp.broadcast_to(obs_lon[:, span], (LANES, LANES)))
            live = lax.broadcasted_iota(jnp.int32, (LANES, LANES), 0) + piece * LANES < count
            for block in range(group // LANES):
                first = m * group + block * LANES
                row = first // lon
                cell_lat = (b * band_rows + row).astype(jnp.float32)
                cell_lon = (first - row * lon).astype(jnp.float32) + lax.broadcasted_iota(
                    jnp.int32, (LANES, LANES), 1
                ).astype(jnp.float32)
                lat_gap = jnp.abs(lat_c - cell_lat)
                lat_gap = jnp.minimum(lat_gap, nlat - lat_gap)
                lon_gap = jnp.abs(lon_c - cell_lon)
                lon_gap = jnp.minimum(lon_gap, lon - lon_gap)
                lat_term = lat_gap * (1.0 / band_rows)
                lon_term = lon_gap * (4.0 / lon)
                decay = jnp.exp(-0.5 * (lat_term * lat_term + lon_term * lon_term)) * gscale
                weight[t, span, block * LANES : (block + 1) * LANES] = jnp.where(
                    live, decay, jnp.zeros_like(decay)
                )

    for d in range(2):
        aux_copy(d).wait_recv()
    for part_at in range(2):
        lead = near_winds * part_at
        for i in range(near_winds):
            wind[part_at, i] = jnp.broadcast_to(0.5 * aux_recv[1, lead + i : lead + i + 1], (SUB, lon))
            wind[part_at, near_winds + band_rows + i] = jnp.broadcast_to(
                0.5 * aux_recv[0, lead + i : lead + i + 1], (SUB, lon)
            )
        for i in range(band_rows):
            wind[part_at, near_winds + i] = jnp.broadcast_to(0.5 * courant[part_at, i : i + 1], (SUB, lon))

    def advect(c):
        for d in range(2):
            halo_copy(d, c).wait_recv()
        for d in range(2):
            for i in range(STEPS):
                at = 2 * near_winds + i
                halo[1 - d, i] = halo_recv[d, c, i].astype(jnp.float32) + aux_recv[d, at : at + 1]

        @pl.loop(0, CHUNK // SUB)
        def _(s):
            span = pl.ds(pl.multiple_of(s * SUB, SUB), SUB)
            q = [halo[0, i, span] for i in range(STEPS)]
            full = pl.ds(pl.multiple_of(c * CHUNK + s * SUB, SUB), SUB)
            q += [adv[row, full] for row in range(band_rows)]
            q += [halo[1, i, span] for i in range(STEPS)]
            for step in range(STEPS):
                new = []
                for i in range(1, len(q) - 1):
                    now, north, south = q[i], q[i - 1], q[i + 1]
                    west = pltpu.roll(now, 1, 1)
                    east = pltpu.roll(now, lon - 1, 1)
                    at = i - 1 + step
                    rise = wind[0, at] * (now - north) + wind[1, at] * (now - west)
                    near4 = (north + south) + (east + west)
                    new.append(
                        (1.0 - 4.0 * DIFFUSION) * now + DIFFUSION * near4 - (1.0 + jnp.tanh(now)) * rise
                    )
                q = new
            for row in range(band_rows):
                adv[row, full] = q[row]

    def pieces():
        for row in range(band_rows):
            for lane in range(0, lon, LANES):
                cell = row * lon + lane
                yield row, slice(lane, lane + LANES), cell // group, cell % group

    def regroup(c):
        full = pl.ds(pl.multiple_of(c * CHUNK, CHUNK), CHUNK)
        for row, lanes, g, at in pieces():
            diff = adv[row, full, lanes] - ref_send[g, :, at : at + LANES]
            group_send[g, c, :, at : at + LANES] = diff.astype(jnp.bfloat16)
        for k in far_first:
            group_copy(c, k).start()

    advect(0)
    for row, lanes, g, at in pieces():
        ref_send[g, :, at : at + LANES] = jnp.mean(adv[row, :CHUNK, lanes], axis=0, keepdims=True)
    for k in range(n_mem):
        ref_copy(k).start()
    regroup(0)

    @pl.loop(1, chunks)
    def _(c):
        advect(c)
        regroup(c)

    loads[5].wait()
    for d in range(2):
        for k in range(1, n_mem):
            spread_copy(d, k).wait_recv()
    for t in range(LIST):
        near_t[t] = jnp.transpose(near[offs[t]])

    for k in range(n_mem):
        copies = [ref_copy(k)] + [group_copy(c, k) for c in range(chunks)]
        for copy in copies:
            copy.wait() if k == 0 else copy.wait_recv()
    average = jnp.zeros((1, group), jnp.float32)
    for j in range(n_mem):
        added = jnp.zeros((CHUNK, group), jnp.float32)
        for c in range(chunks):
            added = added + group_recv[j, c].astype(jnp.float32)
        average = average + jnp.sum(added, axis=0, keepdims=True) + local * ref_recv[j]
    average = average * (1.0 / members)
    for j in range(n_mem):
        shift = ref_recv[j] - average
        for c in range(chunks):
            start = j * local + c * CHUNK
            pert = group_recv[j, c].astype(jnp.float32) + shift
            series[start : start + CHUNK] = pert.astype(jnp.bfloat16)

    def scaled(t, lanes):
        projected = jnp.dot(near[offs[t]], series[:, lanes], preferred_element_type=jnp.float32)
        return (projected * weight[t, :, lanes]).astype(jnp.bfloat16)

    for power in range(1, DEGREE):
        result = None
        for t in range(LIST):
            term = jnp.dot(near_t[t], scaled(t, slice(0, group)), preferred_element_type=jnp.float32)
            result = term if result is None else result + term
        series[...] = result.astype(jnp.bfloat16)
        if power == 1:
            total[...] = COEFFS[power] * result
        else:
            total[...] += COEFFS[power] * result
    for h in range(halves):
        lanes = slice(h * width, (h + 1) * width)
        last = [scaled(t, lanes) for t in range(LIST)]
        for at in reversed(range(n_mem // 2)):
            rows = pl.ds(pl.multiple_of(chips[at] * (2 * local), 2 * local), 2 * local)
            result = None
            for t in range(LIST):
                term = jnp.dot(near_t[t, rows], last[t], preferred_element_type=jnp.float32)
                result = term if result is None else result + term
            result = (total[rows, lanes] + COEFFS[DEGREE] * result).astype(jnp.bfloat16)
            for j in range(2):
                back_send[h, chips[at] * 2 + j] = result[j * local : (j + 1) * local]
            for k in (2 * at + 1, 2 * at):
                back_copy(h, k).start()

    for h in range(halves):
        for k in range(n_mem):
            copy = back_copy(h, k)
            copy.wait() if k == 0 else copy.wait_recv()
        for row, lanes, g, at in pieces():
            if at // width != h:
                continue
            off = at - h * width
            adv[row, :, lanes] += back_recv[h, g, :, off : off + LANES].astype(jnp.float32)

    @pl.loop(0, local // SUB)
    def _(block):
        span = pl.ds(pl.multiple_of(block * SUB, SUB), SUB)
        out[span] = jnp.swapaxes(adv[:, span], 0, 1)

    for d in range(2):
        cell_copy(d).wait_send()
        obs_copy(d).wait_send()
        aux_copy(d).wait_send()
        for c in range(chunks):
            halo_copy(d, c).wait_send()
        for k in range(1, n_mem):
            spread_copy(d, k).wait_send()
    for k in range(1, n_mem):
        ref_copy(k).wait_send()
        for c in range(chunks):
            group_copy(c, k).wait_send()
        for h in range(halves):
            back_copy(h, k).wait_send()


def shards(state, courant, obs_pert, obs_cell, block_rows, band_list):
    local, band_rows, lon = state.shape
    n_band = lax.axis_size("band")
    n_mem = lax.axis_size("mem")
    obs_rows, members = obs_pert.shape[1:]
    group = band_rows * lon // n_mem
    halves = 2 if group >= 4 * LANES else 1
    width = group // halves
    chunks = local // CHUNK
    bf16, f32 = jnp.bfloat16, jnp.float32
    dma = pltpu.SemaphoreType.DMA
    return pl.pallas_call(
        functools.partial(kernel, (n_band, n_mem, local, band_rows, lon, obs_rows, halves)),
        out_shape=pltpu.VMEM(state.shape, f32),
        in_specs=[pl.BlockSpec(memory_space=pltpu.HBM)] * 6,
        out_specs=pl.BlockSpec(memory_space=pltpu.VMEM),
        scratch_shapes=[
            pltpu.VMEM(state.shape, f32),
            pltpu.VMEM(courant.shape, f32),
            pltpu.SMEM(block_rows.shape, jnp.int32),
            pltpu.SMEM(band_list.shape, jnp.int32),
            pltpu.VMEM((3, obs_rows, members), bf16),
            pltpu.VMEM((3, 1, obs_rows), jnp.int32),
            pltpu.VMEM((LIST, members, obs_rows), bf16),
            pltpu.VMEM((LIST, obs_rows, group), f32),
            pltpu.VMEM((2, chunks, STEPS, CHUNK, lon), bf16),
            pltpu.VMEM((2, chunks, STEPS, CHUNK, lon), bf16),
            pltpu.VMEM((2, 16, lon), f32),
            pltpu.VMEM((2, 16, lon), f32),
            pltpu.VMEM((2, STEPS, CHUNK, lon), f32),
            pltpu.VMEM((2, band_rows + 2 * (STEPS - 1), SUB, lon), f32),
            pltpu.VMEM((band_rows, local, lon), f32),
            pltpu.VMEM((n_mem, 1, group), f32),
            pltpu.VMEM((n_mem, 1, group), f32),
            pltpu.VMEM((n_mem, chunks, CHUNK, group), bf16),
            pltpu.VMEM((n_mem, chunks, CHUNK, group), bf16),
            pltpu.VMEM((halves, n_mem, local, width), bf16),
            pltpu.VMEM((halves, n_mem, local, width), bf16),
            pltpu.VMEM((members, group), bf16),
            pltpu.VMEM((members, group), f32),
            dma((2,)), dma((2,)), dma((2,)), dma((2,)),
            dma((2, n_mem)), dma((2, n_mem)),
            dma((2,)), dma((2,)),
            dma((2, chunks)), dma((2, chunks)),
            dma((n_mem,)), dma((n_mem,)),
            dma((chunks, n_mem)), dma((chunks, n_mem)),
            dma((halves, n_mem)), dma((halves, n_mem)),
            dma((6,)),
            dma((local // SUB,)),
        ],
        compiler_params=pltpu.CompilerParams(
            collective_id=0, has_side_effects=True, vmem_limit_bytes=60 * 1024 * 1024
        ),
    )(state, courant, obs_cell, block_rows, band_list, obs_pert)


def solution(mesh):
    return jax.shard_map(
        shards,
        mesh=mesh,
        in_specs=(
            P("mem", "band", None),
            P(None, "band", None),
            P("band", None, None),
            P("band", None),
            P(),
            P("band", None),
        ),
        out_specs=P("mem", "band", None),
        check_vma=False,
    )
```
